32 devices in a mesh: req: 4 (over y, core), blk: 8 (over z, x).
Axes of the slice: x: 2, y: 2, z: 4, core: 2. Of those that a mesh axis runs over, the one named last changes fastest.
Arguments:
- queries: bfloat16 [512, 8192], P('req', 'blk'), may hold values from -120 to 120
- suffix_key_value: bfloat16 [512, 8, 256], P('req'), may hold values from -6 to 6
- residual: bfloat16 [512, 8192], P('req', 'blk'), may hold values from -10 to 10
- gain: float32 [8192], P('blk'), may hold values from 0.1 to 1.9
- gate_up: bfloat16 [8192, 2, 14336], P('blk', None, 'req'), may hold values from -0.0625 to 0.0625
- prefix_cache_slots: bfloat16 [32, 128, 8, 256], P('req'), may hold values from -6 to 6
- prefix_page_slots: int32 [32], replicated, may hold values from 0 to 31, each once
- lengths: int32 [4, 4], replicated, may hold values from 1 to 64, 128 in all within a row
- counts: int32 [4], replicated, may hold values from 1 to 32, as said below
Outputs:
- hidden: bfloat16 [512, 14336], P('blk', 'req')
- suffix_cache: bfloat16 [512, 2048], P('req', 'blk')
The draws below stay inside these ranges and needn't reach their ends.
Inputs may be any that keep to these rules, and one draw needn't show every extreme that they name: `prefix_page_slots`: slot s of prefix_cache_slots lies on index s // 8 of req; every slot holds exactly one page. Each group's lengths sum to 128, and each group has one request of exactly 64 tokens. `counts`: some group reads all 32 pages.
All inputs are finite; a program needn't handle non-finite values.
Results may differ from the reference program's by a relative error of at most 0.034.
Values may be sent and summed in bfloat16 or wider, within the bound.
No kernel may reach another device: no remote copies, remote signals or barrier semaphores. Data moves between devices by JAX's collectives and lax.ppermute only.
A program may use at most 256 MiB of HBM per device.

```python
import math
import jax
import jax.numpy as jnp
import numpy as np
from jax import lax

D = 8192
QUERY_HEADS = 64
KEY_VALUE_HEADS = 8
HEAD_SIZE = 128
FF = 14336
PAGE_TOKENS = 128
RPG = 4
GROUP_TOKENS = 128
GROUPS = 4
SUFFIX_TOKENS = 512
PREFIX_PAGES = 32


def draw_queries(key, part):
    values = jax.random.normal(key, (SUFFIX_TOKENS, QUERY_HEADS * HEAD_SIZE), jnp.float32) * 3.0
    return jnp.clip(values, -120.0, 120.0).astype(jnp.bfloat16)


def draw_residual(key, part):
    rising = 0.5 * jnp.exp(math.log(3.0) * jnp.arange(D, dtype=jnp.float32) / D)
    values = jax.random.normal(key, (SUFFIX_TOKENS, D), jnp.float32) * rising[None, :]
    return jnp.clip(values, -10.0, 10.0).astype(jnp.bfloat16)


def draw_counts(key, part):
    key_vals, key_top = jax.random.split(jax.random.fold_in(key, 7))
    values = jax.random.randint(key_vals, (GROUPS,), 1, PREFIX_PAGES + 1)
    busiest = jax.random.randint(key_top, (), 0, GROUPS)
    return jnp.where(jnp.arange(GROUPS) == busiest, PREFIX_PAGES, values).astype(jnp.int32)


def level_of(stream_key, shape, pieces, least, top_value):
    level = 1.0
    for dim, blocks in pieces:
        heights = jax.random.uniform(jax.random.fold_in(jax.random.fold_in(stream_key, 6), dim), (blocks,), jnp.float32, least / len(pieces), top_value / len(pieces))
        level = level * jnp.repeat(jnp.exp(heights), shape[dim] // blocks).reshape((-1,) + (1,) * (len(shape) - 1 - dim))
    return level


def split_up(number_of, total, reach, lean):
    loads = [(1 << 20) // math.isqrt(standing ** lean) + 1 for standing in range(2, number_of + 1)]
    surplus, given = total - reach - (number_of - 1), [1] * (number_of - 1)
    while surplus > 0:
        free = [i for i in range(number_of - 1) if given[i] < reach]
        pool, budget = sum([loads[i] for i in free]), surplus
        for i in free:
            extra = min(reach - given[i], max(1, budget * loads[i] // pool), surplus)
            given[i] = given[i] + extra
            surplus = surplus - extra
    return np.array([reach] + given)


def uneven_parts(stream_key, amount, total, bound, skew):
    if amount == 2:
        one = jax.random.randint(stream_key, (), max(1, total - bound), min(bound, total - 1) + 1)
        return jnp.stack([one, total - one])
    sizes = jnp.asarray(split_up(amount, total, bound, skew), jnp.int32)
    twos = (amount - 1) // 2
    source_of, taker = sizes[1:1 + 2 * twos:2], sizes[2:2 + 2 * twos:2]
    room = jnp.minimum(source_of - 1, bound - taker)
    passed = jax.random.randint(jax.random.fold_in(stream_key, 1), (twos,), 0, 1 << 20) % (room + 1)
    sizes = sizes.at[1:1 + 2 * twos:2].set(source_of - passed).at[2:2 + 2 * twos:2].set(taker + passed)
    return sizes[jax.random.permutation(jax.random.fold_in(stream_key, 2), amount)]


def centred(own_key, extent, scale, most, shards=(), held_as=jnp.bfloat16):
    array = jax.random.normal(own_key, extent, jnp.float32) * scale
    if len(shards) > 0:
        array = level_of(own_key, extent, shards, -0.22, 0.18) * array
    return jnp.clip(array, min=-most, max=most).astype(held_as)


def setup_inputs(seed: int = 0) -> dict:
    key_of = jax.random.split(jax.random.key(seed), 10)
    queries = draw_queries(jax.random.fold_in(key_of[9], 71), 0)
    suffix_key_value = centred(key_of[1], (SUFFIX_TOKENS, KEY_VALUE_HEADS, 2 * HEAD_SIZE), 1.0, 6.0, ((0, 4),))
    residual = draw_residual(jax.random.fold_in(key_of[9], 71), 0)
    gain = jnp.clip(1.0 + 0.18 * jax.random.normal(key_of[3], (D,), jnp.float32), 0.1, 1.9)
    gate_up = centred(key_of[4], (D, 2, FF), D ** -0.5, 0.0625, ((0, 8), (2, 4)))
    prefix_cache_slots = centred(key_of[5], (PREFIX_PAGES, PAGE_TOKENS, KEY_VALUE_HEADS, 2 * HEAD_SIZE), 1.0, 6.0, ((0, 4),))
    prefix_page_slots = jax.random.permutation(key_of[6], PREFIX_PAGES).astype(jnp.int32)
    lengths = jax.vmap(lambda own: uneven_parts(own, RPG, GROUP_TOKENS, GROUP_TOKENS // 2, 2))(jax.random.split(key_of[7], GROUPS)).reshape((GROUPS, RPG)).astype(jnp.int32)
    counts = draw_counts(jax.random.fold_in(key_of[9], 71), 0)
    return {"queries": queries, "suffix_key_value": suffix_key_value, "residual": residual, "gain": gain, "gate_up": gate_up, "prefix_cache_slots": prefix_cache_slots, "prefix_page_slots": prefix_page_slots, "lengths": lengths, "counts": counts}


NEGATIVE = -1e+30
EPSILON = 1e-05
ROPE_BASE = 500000.0

def rope_tables(positions, half_dim):
    inverse = jnp.exp(-math.log(ROPE_BASE) * jnp.arange(half_dim, dtype=jnp.float32) * 2.0 / (2 * half_dim))
    angles = positions.astype(jnp.float32)[:, None] * inverse[None, :]
    return (jnp.cos(angles), jnp.sin(angles))

def rotate(vectors, cosines, sines):
    half_dim = vectors.shape[-1] // 2
    lower = vectors[..., :half_dim]
    upper = vectors[..., half_dim:]
    return jnp.concatenate([lower * cosines - upper * sines, upper * cosines + lower * sines], -1)

def suffix_layout(lengths_row, page_count, group_len, page_len):
    starts = (jnp.cumsum(lengths_row) - lengths_row).astype(jnp.int32)
    tokens_at = jnp.arange(group_len, dtype=jnp.int32)
    request = (lax.optimization_barrier(jnp.sum((tokens_at[:, None] >= starts[None, :]).astype(jnp.int32), 1)) - 1).astype(jnp.int32)
    slots_req = jnp.arange(lengths_row.shape[0], dtype=jnp.int32)
    request_begin = lax.optimization_barrier(jnp.sum(jnp.where(request[:, None] == slots_req[None, :], starts[None, :], 0), 1)).astype(jnp.int32)
    offset = (tokens_at - request_begin).astype(jnp.int32)
    return (request, offset, (page_count * page_len + offset).astype(jnp.int32))

def reference(queries, suffix_key_value, residual, gain, gate_up, prefix_cache_slots, prefix_page_slots, lengths, counts):
    heads_per_group = QUERY_HEADS // KEY_VALUE_HEADS
    score_scale = 1.0 / math.sqrt(HEAD_SIZE)
    sorted_rows = prefix_cache_slots[prefix_page_slots].reshape(PREFIX_PAGES * PAGE_TOKENS, KEY_VALUE_HEADS, 2 * HEAD_SIZE)
    prefix_keys = sorted_rows[:, :, :HEAD_SIZE].astype(jnp.float32)
    prefix_values = sorted_rows[:, :, HEAD_SIZE:].astype(jnp.float32)
    key_index = jnp.arange(PREFIX_PAGES * PAGE_TOKENS, dtype=jnp.int32)

    def one_group(group_index):
        query_rows = lax.dynamic_slice_in_dim(queries, group_index * GROUP_TOKENS, GROUP_TOKENS, 0)
        fresh_rows = lax.dynamic_slice_in_dim(suffix_key_value, group_index * GROUP_TOKENS, GROUP_TOKENS, 0)
        page_count = counts[group_index]
        request, offset, positions = suffix_layout(lengths[group_index], page_count, GROUP_TOKENS, PAGE_TOKENS)
        cosines, sines = rope_tables(positions, HEAD_SIZE // 2)
        rotated_query = rotate(query_rows.astype(jnp.float32).reshape(GROUP_TOKENS, QUERY_HEADS, HEAD_SIZE), cosines[:, None], sines[:, None]).astype(jnp.bfloat16)
        keys_new = rotate(fresh_rows[:, :, :HEAD_SIZE].astype(jnp.float32), cosines[:, None], sines[:, None]).astype(jnp.bfloat16)
        values_new = fresh_rows[:, :, HEAD_SIZE:]
        query_float32 = rotated_query.astype(jnp.float32).reshape(GROUP_TOKENS, KEY_VALUE_HEADS, heads_per_group, HEAD_SIZE)
        prefix_scores = jnp.einsum('tkgd,nkd->kgtn', query_float32, prefix_keys) * score_scale
        suffix_scores = jnp.einsum('tkgd,skd->kgts', query_float32, keys_new.astype(jnp.float32)) * score_scale
        prefix_ok = (key_index < page_count * PAGE_TOKENS)[None, None, None, :]
        suffix_ok = ((request[:, None] == request[None, :]) & (offset[None, :] <= offset[:, None]))[None, None]
        prefix_scores = jnp.where(prefix_ok, prefix_scores, NEGATIVE)
        suffix_scores = jnp.where(suffix_ok, suffix_scores, NEGATIVE)
        row_max = jnp.maximum(lax.optimization_barrier(jnp.max(prefix_scores, -1)), lax.optimization_barrier(jnp.max(suffix_scores, -1)))
        prefix_probs = jnp.where(prefix_ok, jnp.exp(prefix_scores - row_max[..., None]), 0.0)
        suffix_probs = jnp.where(suffix_ok, jnp.exp(suffix_scores - row_max[..., None]), 0.0)
        row_sum = lax.optimization_barrier(jnp.sum(prefix_probs, -1)) + lax.optimization_barrier(jnp.sum(suffix_probs, -1))
        weighted = jnp.einsum('kgtn,nkd->tkgd', prefix_probs.astype(jnp.bfloat16).astype(jnp.float32), prefix_values)
        weighted = weighted + jnp.einsum('kgts,skd->tkgd', suffix_probs.astype(jnp.bfloat16).astype(jnp.float32), values_new.astype(jnp.float32))
        attention_output = weighted / jnp.transpose(row_sum, (2, 0, 1))[..., None]
        updated_cache = jnp.concatenate([keys_new, values_new], -1)
        return (attention_output.reshape(GROUP_TOKENS, QUERY_HEADS * HEAD_SIZE), updated_cache.reshape(GROUP_TOKENS, 2 * KEY_VALUE_HEADS * HEAD_SIZE))
    attended_all, cache_list = lax.map(one_group, jnp.arange(GROUPS, dtype=jnp.int32))
    attended_all = attended_all.reshape(SUFFIX_TOKENS, D)
    stream = (residual.astype(jnp.float32) + attended_all).astype(jnp.bfloat16)
    stream_f32 = stream.astype(jnp.float32)
    mean_square = lax.optimization_barrier(jnp.mean(stream_f32 * stream_f32, 1, keepdims=True))
    normed = (stream_f32 * lax.rsqrt(mean_square + EPSILON) * gain.astype(jnp.float32)[None, :]).astype(jnp.bfloat16)
    gate_up_sum = jnp.dot(normed, gate_up.reshape(D, 2 * FF), preferred_element_type=jnp.float32)
    hidden = (jax.nn.silu(gate_up_sum[:, :FF]) * gate_up_sum[:, FF:]).astype(jnp.bfloat16)
    return (hidden, cache_list.reshape(SUFFIX_TOKENS, 2 * KEY_VALUE_HEADS * HEAD_SIZE))
```

```python
import functools
import math

import jax
import jax.numpy as jnp
from jax import lax
from jax.experimental import pallas as pl
from jax.experimental.pallas import tpu as pltpu
from jax.sharding import PartitionSpec as P

D = 8192


NEGATIVE = -1e30
EPSILON = 1e-05
ROPE_BASE = 500000.0
ROW_BLOCK = 256
CHUNKS = ((6, (0, 2, 1)), (6, (1, 0, 2)), (6, (0, 2, 1)), (4, (1, 0, 2)), (4, (0, 1, 2)), (2, (1, 0, 2)))
STEPS = ("S0", "S1", "S2", "S3", "S4", "K0", "K1", "S5", "K2", "K3", "K4", "A0", "A1", "K5", "Q0", "A2", "A3", "Q1", "A4", "A5", "Q2", "F0", "F1", "F2", "F3", "F4", "F5")


def rope_tables(positions, half_dim):
    inverse = jnp.exp(
        -math.log(ROPE_BASE) * jnp.arange(half_dim, dtype=jnp.float32) * 2.0 / (2 * half_dim)
    )
    angles = positions.astype(jnp.float32)[:, None] * inverse[None, :]
    cosines, sines = jnp.cos(angles), jnp.sin(angles)
    return (jnp.concatenate([cosines, cosines], 1), jnp.concatenate([-sines, sines], 1))


def suffix_layout(lengths_row, page_count, group_len, page_len):
    starts = jnp.cumsum(lengths_row) - lengths_row
    tokens_at = jnp.arange(group_len, dtype=jnp.int32)
    request = jnp.sum((tokens_at[:, None] >= starts[None, :]).astype(jnp.int32), 1) - 1
    slots_req = jnp.arange(lengths_row.shape[0], dtype=jnp.int32)
    request_begin = jnp.sum(
        jnp.where(request[:, None] == slots_req[None, :], starts[None, :], 0), 1
    )
    offset = tokens_at - request_begin
    return (request, offset, page_count * page_len + offset)


def dot_nt(a, b):
    return lax.dot_general(a, b, (((1,), (1,)), ((), ())), preferred_element_type=jnp.float32)


def rotate(vectors, cosines, signed_sines):
    half_dim = vectors.shape[-1] // 2
    return vectors * cosines + pltpu.roll(vectors, half_dim, 1) * signed_sines


def absorb(items, query, scale, acc, top, total):
    def scores_of(item):
        rows, keys, _, bias = item
        scores = dot_nt(query[rows, :], keys()) * scale
        return scores if bias is None else scores + bias

    scores = scores_of(items[0])
    for i, (rows, _, values, _) in enumerate(items):
        ahead = scores_of(items[i + 1]) if i + 1 < len(items) else None
        old_top = top[rows, :]
        new_top = jnp.maximum(old_top, jnp.max(scores, 1, keepdims=True))
        weights = jnp.exp2(scores - new_top[:, :1])
        factor = jnp.exp2(old_top - new_top)
        top[rows, :] = new_top
        lanes = top.shape[1]
        part = weights[:, :lanes]
        for begin in range(lanes, weights.shape[1], lanes):
            part = part + weights[:, begin : begin + lanes]
        total[rows, :] = total[rows, :] * factor + part
        acc[rows, :] = acc[rows, :] * factor + jnp.dot(
            weights.astype(jnp.bfloat16), values(), preferred_element_type=jnp.float32
        )
        scores = ahead


def absorb_pages(shards, meta, page_len, query, scale, acc, top, total):
    head_dim = query.shape[1]
    rows = query.shape[0]
    row_step = min(ROW_BLOCK, rows)
    keys_here = shards[0].shape[0]
    pages = keys_here // page_len
    count = meta[0]
    visible = [meta[1 + i] < count for i in range(len(shards) * pages)]
    every = functools.reduce(jnp.logical_and, visible)

    def items_of(shard, begin, length, bias):
        return [
            (
                pl.ds(r, row_step),
                lambda: shard[pl.ds(begin, length), :head_dim],
                lambda: shard[pl.ds(begin, length), head_dim:],
                bias,
            )
            for r in range(0, rows, row_step)
        ]

    @pl.when(every)
    def _():
        items = []
        for shard in shards:
            items += items_of(shard, 0, keys_here, None)
        absorb(items, query, scale, acc, top, total)

    per_block = min(4, pages)
    length = per_block * page_len
    lane = lax.broadcasted_iota(jnp.int32, (1, length), 1) // page_len
    for s, shard in enumerate(shards):
        for begin in range(0, pages, per_block):
            seen = visible[s * pages + begin : s * pages + begin + per_block]

            @pl.when(jnp.logical_not(every) & functools.reduce(jnp.logical_or, seen))
            def _():
                bias = jnp.zeros((1, length), jnp.float32)
                for i in range(per_block):
                    bias = jnp.where((lane == i) & jnp.logical_not(seen[i]), NEGATIVE, bias)
                items = items_of(shard, begin * page_len, length, bias)
                absorb(items, query, scale, acc, top, total)


def first_kernel(shards, heads, head_dim, page_len, scale, *refs):
    meta, queries, own, cosines, sines, mask = refs[:6]
    kv = refs[6 : 6 + shards]
    query, acc, top, total, cache = refs[6 + shards :]
    group_len = queries.shape[0]
    cos, sin = cosines[...], sines[...]
    keys_new = rotate(own[:, :head_dim].astype(jnp.float32), cos, sin).astype(jnp.bfloat16)
    cache[:, :head_dim] = keys_new
    cache[:, head_dim:] = own[:, head_dim:]
    for h in range(heads):
        vectors = queries[:, h * head_dim : (h + 1) * head_dim].astype(jnp.float32)
        query[pl.ds(h * group_len, group_len), :] = rotate(vectors, cos, sin).astype(jnp.bfloat16)
    acc[...] = jnp.zeros_like(acc)
    total[...] = jnp.zeros_like(total)
    top[...] = jnp.full(top.shape, NEGATIVE, jnp.float32)
    items = [
        (
            pl.ds(h * group_len, group_len),
            lambda: cache[:, :head_dim],
            lambda: cache[:, head_dim:],
            mask[...],
        )
        for h in range(heads)
    ]
    absorb(items, query, scale, acc, top, total)
    absorb_pages(kv, meta, page_len, query, scale, acc, top, total)


def rest_kernel(shards, heads, head_dim, page_len, scale, *refs):
    meta, query, acc_in, top_in, total_in, residual = refs[:6]
    kv = refs[6 : 6 + shards]
    stream, acc, top, total = refs[6 + shards :]
    group_len = residual.shape[0]
    acc[...] = acc_in[...]
    top[...] = top_in[...]
    total[...] = total_in[...]
    absorb_pages(kv, meta, page_len, query, scale, acc, top, total)
    for h in range(heads):
        at = pl.ds(h * group_len, group_len)
        lanes = slice(h * head_dim, (h + 1) * head_dim)
        attended = acc[at, :] / jnp.sum(total[at, :], 1, keepdims=True)
        stream[:, lanes] = (residual[:, lanes].astype(jnp.float32) + attended).astype(jnp.bfloat16)


def spread(vectors, lane):
    rows, depth = vectors.shape
    step = 128
    source = lax.broadcasted_iota(jnp.int32, (step, 2 * step), 0)
    target = lax.broadcasted_iota(jnp.int32, (step, 2 * step), 1)
    place = jnp.where(target == 2 * source + lane, 1.0, 0.0).astype(jnp.bfloat16)
    return [
        jnp.dot(vectors[:, k : k + step], place, preferred_element_type=jnp.float32).astype(
            jnp.bfloat16
        )
        for k in range(0, depth, step)
    ]


def lhs_kernel(parts, blocks, *refs):
    meta, gain = refs[:2]
    streams = refs[2 : 2 + parts]
    lhs, squares, held = refs[2 + parts :]
    per_part = blocks // parts if blocks > parts else 1
    block_len = held.shape[1]
    for j, stream in enumerate(streams):
        for i in range(per_part):
            held[meta[1 + j] * per_part + i] = stream[pl.ds(i * block_len, block_len), :]
    for p in range(blocks):
        vectors = held[lax.bitwise_xor(meta[0], blocks - 1 - p)].astype(jnp.float32)
        square = jnp.sum(vectors * vectors, 1, keepdims=True)
        squares[pl.ds(p, 1), :] = jnp.broadcast_to(square, (block_len, 128)).T[:1, :]
        scaled = (vectors * gain[...]).astype(jnp.bfloat16)
        for half in range(2):
            for i, piece in enumerate(spread(scaled, half)):
                lhs[half, p, :, i * 256 : (i + 1) * 256] = piece


def send_kernel(lhs, weights, out):
    product = times(lhs, weights)
    out[...] = product.astype(jnp.bfloat16).reshape(out.shape)


def keep_kernel(axis, lhs, weights, got, send, keep):
    product = times(lhs, weights).reshape(got.shape)
    summed = (product + got[...].astype(jnp.float32)).astype(jnp.bfloat16)
    high, low = send.shape[1], send.shape[2]
    summed = summed.reshape((2, high, 2, low) + got.shape[-2:])
    send[...] = summed[:, :, 0]
    keep[...] = summed[:, :, 1]


def times(lhs, weights):
    depth = lhs.shape[-1]
    return jnp.dot(
        lhs[...].reshape(-1, depth),
        weights[...].reshape(depth, weights.shape[-1]),
        preferred_element_type=jnp.float32,
    )


def vmem_call(kernel, n_in, out_shape, scratch, flops):
    whole = pl.BlockSpec(memory_space=pltpu.VMEM)
    return pl.pallas_call(
        kernel,
        in_specs=[pl.BlockSpec(memory_space=pltpu.SMEM)] + [whole] * n_in,
        out_specs=jax.tree.map(lambda _: whole, out_shape),
        out_shape=out_shape,
        scratch_shapes=scratch,
        compiler_params=pltpu.CompilerParams(vmem_limit_bytes=48 << 20),
        cost_estimate=pl.CostEstimate(flops=1, bytes_accessed=1, transcendentals=0),
    )


def gather_near(own, size, index):
    twin = [(r, r ^ 1) for r in range(size)]
    far = []
    for shift in range(1, size // 2):
        pairs = [(r, (r + 2 * shift) % size) for r in range(size)]
        far.append((lax.ppermute(own, "req", pairs), (index - 2 * shift) % size))
    return [(own, index), (lax.ppermute(own, "req", twin), index ^ 1)], far


def gather_far(far, size):
    twin = [(r, r ^ 1) for r in range(size)]
    return far + [(lax.ppermute(part, "req", twin), origin ^ 1) for part, origin in far]


def on_device(
    queries,
    suffix_key_value,
    residual,
    gain,
    gate_up,
    prefix_cache_slots,
    prefix_page_slots,
    lengths,
    counts,
):
    blocks = lax.axis_size("blk")
    groups = lax.axis_size("req")
    column = lax.axis_index("blk")
    group_index = lax.axis_index("req")
    group_len = queries.shape[0]
    heads_kv = suffix_key_value.shape[1]
    head_dim = suffix_key_value.shape[2] // 2
    heads_here = queries.shape[1] // head_dim
    slots_here, page_len = prefix_cache_slots.shape[:2]
    score_scale = math.log2(math.e) / math.sqrt(head_dim)
    kv_head = column * heads_kv // blocks
    page_count = counts[group_index]

    own_slots = lax.dynamic_index_in_dim(prefix_cache_slots, kv_head, 2, keepdims=False)
    own_slots = own_slots.reshape(slots_here * page_len, 2 * head_dim)
    near, far = gather_near(own_slots, groups, group_index)

    request, offset, positions = suffix_layout(
        lengths[group_index], page_count, group_len, page_len
    )
    cosines, sines = rope_tables(positions, head_dim // 2)
    own_head = lax.dynamic_index_in_dim(suffix_key_value, kv_head, 1, keepdims=False)
    allowed = (request[:, None] == request[None, :]) & (offset[None, :] <= offset[:, None])
    mask = jnp.where(allowed, 0.0, NEGATIVE).astype(jnp.float32)

    pages_total = prefix_page_slots.shape[0]
    page_ids = jnp.arange(pages_total, dtype=jnp.int32)
    match = prefix_page_slots[None, :] == page_ids[:, None]
    page_of_slot = jnp.sum(jnp.where(match, page_ids[None, :], 0), 1).reshape(groups, slots_here)

    def meta(parts):
        ids = [lax.dynamic_index_in_dim(page_of_slot, o, 0, keepdims=False) for _, o in parts]
        return jnp.concatenate([page_count[None]] + ids)

    rows = heads_here * group_len
    state = (
        jax.ShapeDtypeStruct((rows, head_dim), jnp.float32),
        jax.ShapeDtypeStruct((rows, head_dim), jnp.float32),
        jax.ShapeDtypeStruct((rows, head_dim), jnp.float32),
    )
    key_flops = 4 * rows * head_dim * slots_here * page_len
    query, acc, top, total, both_new = vmem_call(
        functools.partial(first_kernel, len(near), heads_here, head_dim, page_len, score_scale),
        5 + len(near),
        (jax.ShapeDtypeStruct((rows, head_dim), jnp.bfloat16),)
        + state
        + (jax.ShapeDtypeStruct((group_len, 2 * head_dim), jnp.bfloat16),),
        [],
        key_flops * len(near),
    )(meta(near), queries, own_head, cosines, sines, mask, *[part for part, _ in near])
    arrived = lax.optimization_barrier(([part for part, _ in far], top))[0]
    far = gather_far([(part, origin) for part, (_, origin) in zip(arrived, far)], groups)
    stream = vmem_call(
        functools.partial(rest_kernel, len(far), heads_here, head_dim, page_len, score_scale),
        5 + len(far),
        jax.ShapeDtypeStruct((group_len, heads_here * head_dim), jnp.bfloat16),
        [pltpu.VMEM((rows, head_dim), jnp.float32)] * 3,
        key_flops * len(far),
    )(meta(far), query, acc, top, total, residual, *[part for part, _ in far])

    lane_width = 2 * heads_kv * head_dim // blocks
    updated_cache = lax.dynamic_slice_in_dim(
        both_new, column * lane_width % (2 * head_dim), lane_width, 1
    )

    near, far = gather_near(stream, groups, group_index)
    streams = near + gather_far(far, groups)
    features = stream.shape[1]
    bits = blocks.bit_length() - 1
    block_len = groups * group_len // blocks
    lhs, squares = vmem_call(
        functools.partial(lhs_kernel, groups, blocks),
        1 + groups,
        (
            jax.ShapeDtypeStruct((2, blocks, block_len, 2 * features), jnp.bfloat16),
            jax.ShapeDtypeStruct((blocks, block_len), jnp.float32),
        ),
        [pltpu.VMEM((blocks, block_len, features), jnp.bfloat16)],
        8 * groups * group_len * features * 128,
    )(
        jnp.stack([column] + [origin for _, origin in streams]),
        gain[None, :],
        *[part for part, _ in streams],
    )

    def swap(array, bit):
        return lax.ppermute(array, "blk", [(b, b ^ (1 << bit)) for b in range(blocks)])

    def halves(array, bit, left, lead):
        low = sum(1 for other in left if other < bit)
        shape = array.shape[:lead] + (-1, 2, 1 << low) + array.shape[lead + 1 :]
        split = array.reshape(shape)
        out = array.shape[:lead] + (-1,) + array.shape[lead + 1 :]
        return [
            lax.index_in_dim(split, i, lead + 1, keepdims=False).reshape(out) for i in range(2)
        ]

    def add(keep, got):
        return (keep.astype(jnp.float32) + got.astype(jnp.float32)).astype(keep.dtype)

    def multiply(which, bit, begin, end, lhs, got=None, next_bit=None):
        width = end - begin
        tile = 128 * math.gcd(math.gcd(begin // 128, width // 128), 2)
        low = 1 << bit
        high = blocks // (2 * low)
        rows = lhs.reshape(2, high, 2, low, block_len, 2 * features)
        in_specs = [
            pl.BlockSpec(
                (2, high, None, low, block_len, 2 * features), lambda j: (0, 0, which, 0, 0, 0)
            ),
            pl.BlockSpec((features, 2, tile), lambda j: (0, 0, begin // tile + j)),
        ]
        operands = [rows, gate_up]
        if got is None:
            kernel = send_kernel
            out = (2, high * low, block_len, width)
            out_specs = pl.BlockSpec(out[:-1] + (tile,), lambda j: (0, 0, 0, j))
            out_shape = jax.ShapeDtypeStruct(out, jnp.bfloat16)
        else:
            rest = [other for other in range(bits) if other != bit]
            next_low = 1 << sum(1 for other in rest if other < next_bit)
            next_high = high * low // (2 * next_low)
            out = (2, next_high, next_low, block_len, width)
            spec = pl.BlockSpec(out[:-1] + (tile,), lambda j: (0, 0, 0, 0, j))
            kernel = functools.partial(keep_kernel, None)
            in_specs.append(
                pl.BlockSpec((2, high * low, block_len, tile), lambda j: (0, 0, 0, j))
            )
            operands.append(got)
            out_specs = (spec, spec)
            out_shape = (jax.ShapeDtypeStruct(out, jnp.bfloat16),) * 2
        result = pl.pallas_call(
            kernel,
            grid=(width // tile,),
            in_specs=in_specs,
            out_specs=out_specs,
            out_shape=out_shape,
            compiler_params=pltpu.CompilerParams(vmem_limit_bytes=48 << 20),
            cost_estimate=pl.CostEstimate(flops=1, bytes_accessed=1, transcendentals=0),
        )(*operands)
        if got is None:
            return result
        return [part.reshape((2, -1, block_len, width)) for part in result]

    width_here = gate_up.shape[2]
    units = width_here // 128
    whole_units = sum(size for size, _ in CHUNKS)
    bounds, so_far = [0], 0
    for size, _ in CHUNKS:
        so_far += size
        bounds.append(128 * max(bounds[-1] // 128 + 1, units * so_far // whole_units))
    orders = [list(order) + list(range(len(order), bits)) for _, order in CHUNKS]

    pieces = [None] * len(CHUNKS)
    flying, kept, lefts = {}, {}, {}
    square_sum, square_keep, square_left = squares, None, list(range(bits))
    token = squares

    def after(array):
        return lax.optimization_barrier((array, token))[0]

    for step in STEPS:
        kind, c = step[0], int(step[1:])
        if kind == "Q":
            if c == 0:
                square_sum = after(squares)
            else:
                square_sum = add(after(square_keep), flying["Q"])
                square_left.remove(c - 1)
            for bit in [c] if c < 2 else range(c, bits):
                if bit > c:
                    square_sum = add(square_keep, flying["Q"])
                    square_left.remove(bit - 1)
                send, square_keep = halves(square_sum, bit, square_left, 0)
                flying["Q"] = swap(send, bit)
            token = square_sum
            continue
        begin, end, order = bounds[c], bounds[c + 1], orders[c]
        if kind == "S":
            send = multiply(0, order[0], begin, end, after(lhs))
            lefts[c] = list(range(bits))
            flying[c] = swap(send, order[0])
            token = send
        elif kind == "K":
            send, kept[c] = multiply(1, order[0], begin, end, lhs, after(flying[c]), order[1])
            lefts[c].remove(order[0])
            flying[c] = swap(send, order[1])
            token = send
        elif kind == "A":
            for n in range(2, bits):
                summed = add(after(kept[c]), flying[c])
                lefts[c].remove(order[n - 1])
                send, kept[c] = halves(summed, order[n], lefts[c], 1)
                flying[c] = swap(send, order[n])
            token = send
        else:
            summed = after(kept[c]).astype(jnp.float32) + flying[c].astype(jnp.float32)
            norm = lax.rsqrt(
                (square_keep + flying["Q"]).reshape(block_len, 1) / D + EPSILON
            )
            summed = summed.reshape(2, block_len, end - begin) * norm
            pieces[c] = (jax.nn.silu(summed[0]) * summed[1]).astype(jnp.bfloat16)
            token = pieces[c]
    return (jnp.concatenate(pieces, 1), updated_cache)


def solution(mesh):
    placed = (
        P("req", "blk"),
        P("req", None, None),
        P("req", "blk"),
        P("blk"),
        P("blk", None, "req"),
        P("req", None, None, None),
        P(),
        P(),
        P(),
    )
    return jax.shard_map(
        on_device,
        mesh=mesh,
        in_specs=placed,
        out_specs=(P("blk", "req"), P("req", "blk")),
        check_vma=False,
    )
```

```python
import functools
import math

import jax
import jax.numpy as jnp
from jax import lax
from jax.experimental import pallas as pl
from jax.experimental.pallas import tpu as pltpu
from jax.sharding import PartitionSpec as P

D = 8192


NEGATIVE = -1e30
EPSILON = 1e-05
ROPE_BASE = 500000.0
ROW_BLOCK = 256
CHUNKS = ((6, (0, 2, 1)), (6, (1, 0, 2)), (6, (0, 2, 1)), (4, (1, 0, 2)), (4, (0, 1, 2)), (2, (1, 0, 2)))
STEPS = ("S0", "S1", "S2", "S3", "S4", "K0", "K1", "S5", "K2", "K3", "K4", "A0", "A1", "K5", "Q0", "A2", "A3", "Q1", "A4", "A5", "Q2", "F0", "F1", "F2", "F3", "F4", "F5")


def rope_tables(positions, half_dim):
    inverse = jnp.exp(
        -math.log(ROPE_BASE) * jnp.arange(half_dim, dtype=jnp.float32) * 2.0 / (2 * half_dim)
    )
    angles = positions.astype(jnp.float32)[:, None] * inverse[None, :]
    cosines, sines = jnp.cos(angles), jnp.sin(angles)
    return (jnp.concatenate([cosines, cosines], 1), jnp.concatenate([-sines, sines], 1))


def suffix_layout(lengths_row, page_count, group_len, page_len):
    starts = jnp.cumsum(lengths_row) - lengths_row
    tokens_at = jnp.arange(group_len, dtype=jnp.int32)
    request = jnp.sum((tokens_at[:, None] >= starts[None, :]).astype(jnp.int32), 1) - 1
    slots_req = jnp.arange(lengths_row.shape[0], dtype=jnp.int32)
    request_begin = jnp.sum(
        jnp.where(request[:, None] == slots_req[None, :], starts[None, :], 0), 1
    )
    offset = tokens_at - request_begin
    return (request, offset, page_count * page_len + offset)


def dot_nt(a, b):
    return lax.dot_general(a, b, (((1,), (1,)), ((), ())), preferred_element_type=jnp.float32)


def rotate(vectors, cosines, signed_sines):
    half_dim = vectors.shape[-1] // 2
    return vectors * cosines + pltpu.roll(vectors, half_dim, 1) * signed_sines


def absorb(items, query, scale, acc, top, total):
    def scores_of(item):
        rows, pieces = item
        scores = [dot_nt(query[rows, :], keys()) * scale for keys, _, _ in pieces]
        return [s if piece[2] is None else s + piece[2] for s, piece in zip(scores, pieces)]

    scores = scores_of(items[0])
    for i, (rows, pieces) in enumerate(items):
        ahead = scores_of(items[i + 1]) if i + 1 < len(items) else None
        old_top = top[rows, :]
        lanes = old_top.shape[1]
        highest = functools.reduce(
            jnp.maximum,
            [s[:, at : at + lanes] for s in scores for at in range(0, s.shape[1], lanes)],
        )
        new_top = jnp.maximum(old_top, jnp.max(highest, 1, keepdims=True))
        factor = jnp.exp2(old_top - new_top)
        top[rows, :] = new_top
        weights = [jnp.exp2(s - new_top[:, :1]) for s in scores]
        part = sum(w[:, at : at + lanes] for w in weights for at in range(0, w.shape[1], lanes))
        total[rows, :] = total[rows, :] * factor + part
        acc[rows, :] = acc[rows, :] * factor + sum(
            jnp.dot(w.astype(jnp.bfloat16), values(), preferred_element_type=jnp.float32)
            for w, (_, values, _) in zip(weights, pieces)
        )
        scores = ahead


def piece_of(ref, begin, length, bias):
    head_dim = ref.shape[1] // 2
    at = pl.ds(begin, length)
    return (lambda: ref[at, :head_dim], lambda: ref[at, head_dim:], bias)


def absorb_pages(shards, meta, page_len, query, scale, acc, top, total, extra=None):
    rows = query.shape[0]
    row_step = min(ROW_BLOCK, rows)
    parts = [ref for shard in shards for ref in shard]
    pages = parts[0].shape[0] // page_len
    count = meta[0]
    visible = [meta[1 + i] < count for i in range(len(parts) * pages)]
    every = functools.reduce(jnp.logical_and, visible)
    blocks = [pl.ds(r, row_step) for r in range(0, rows, row_step)]

    @pl.when(every)
    def _():
        items = []
        for s, shard in enumerate(shards):
            pieces = [piece_of(ref, 0, ref.shape[0], None) for ref in shard]
            if s == 0 and extra is not None:
                pieces = [extra] + pieces
            items += [(at, pieces) for at in blocks]
        absorb(items, query, scale, acc, top, total)

    if extra is not None:

        @pl.when(jnp.logical_not(every))
        def _():
            absorb([(at, [extra]) for at in blocks], query, scale, acc, top, total)

    per_block = min(4, pages)
    length = per_block * page_len
    lane = lax.broadcasted_iota(jnp.int32, (1, length), 1) // page_len
    for p, part in enumerate(parts):
        for begin in range(0, pages, per_block):
            seen = visible[p * pages + begin : p * pages + begin + per_block]

            @pl.when(jnp.logical_not(every) & functools.reduce(jnp.logical_or, seen))
            def _():
                bias = jnp.zeros((1, length), jnp.float32)
                for i in range(per_block):
                    bias = jnp.where((lane == i) & jnp.logical_not(seen[i]), NEGATIVE, bias)
                piece = piece_of(part, begin * page_len, length, bias)
                absorb([(at, [piece]) for at in blocks], query, scale, acc, top, total)


def grouped(refs, halves):
    return [refs[i : i + halves] for i in range(0, len(refs), halves)]


def first_kernel(parts, halves, heads, head_dim, page_len, scale, *refs):
    meta, queries, own, cosines, sines, mask = refs[:6]
    kv = grouped(refs[6 : 6 + parts], halves)
    query, acc, top, total, cache = refs[6 + parts :]
    group_len = queries.shape[0]
    cos, sin = cosines[...], sines[...]
    keys_new = rotate(own[:, :head_dim].astype(jnp.float32), cos, sin).astype(jnp.bfloat16)
    cache[:, :head_dim] = keys_new
    cache[:, head_dim:] = own[:, head_dim:]
    for h in range(heads):
        vectors = queries[:, h * head_dim : (h + 1) * head_dim].astype(jnp.float32)
        query[pl.ds(h * group_len, group_len), :] = rotate(vectors, cos, sin).astype(jnp.bfloat16)
    acc[...] = jnp.zeros_like(acc)
    total[...] = jnp.zeros_like(total)
    top[...] = jnp.full(top.shape, NEGATIVE, jnp.float32)
    repeats = min(ROW_BLOCK, heads * group_len) // group_len
    bias = jnp.concatenate([mask[...]] * repeats, 0)
    suffix = piece_of(cache, 0, group_len, bias)
    absorb_pages(kv, meta, page_len, query, scale, acc, top, total, suffix)


def rest_kernel(parts, halves, heads, head_dim, page_len, scale, *refs):
    meta, query, acc_in, top_in, total_in, residual = refs[:6]
    kv = grouped(refs[6 : 6 + parts], halves)
    stream, acc, top, total = refs[6 + parts :]
    group_len = residual.shape[0]
    acc[...] = acc_in[...]
    top[...] = top_in[...]
    total[...] = total_in[...]
    absorb_pages(kv, meta, page_len, query, scale, acc, top, total)
    for h in range(heads):
        at = pl.ds(h * group_len, group_len)
        lanes = slice(h * head_dim, (h + 1) * head_dim)
        attended = acc[at, :] / jnp.sum(total[at, :], 1, keepdims=True)
        stream[:, lanes] = (residual[:, lanes].astype(jnp.float32) + attended).astype(jnp.bfloat16)


def spread(vectors, lane):
    rows, depth = vectors.shape
    step = 128
    source = lax.broadcasted_iota(jnp.int32, (step, 2 * step), 0)
    target = lax.broadcasted_iota(jnp.int32, (step, 2 * step), 1)
    place = jnp.where(target == 2 * source + lane, 1.0, 0.0).astype(jnp.bfloat16)
    return [
        jnp.dot(vectors[:, k : k + step], place, preferred_element_type=jnp.float32).astype(
            jnp.bfloat16
        )
        for k in range(0, depth, step)
    ]


def lhs_kernel(parts, blocks, *refs):
    meta, gain = refs[:2]
    streams = refs[2 : 2 + parts]
    lhs, squares, held = refs[2 + parts :]
    per_part = blocks // parts if blocks > parts else 1
    block_len = held.shape[1]
    for j, stream in enumerate(streams):
        for i in range(per_part):
            held[meta[1 + j] * per_part + i] = stream[pl.ds(i * block_len, block_len), :]
    for p in range(blocks):
        vectors = held[lax.bitwise_xor(meta[0], blocks - 1 - p)].astype(jnp.float32)
        square = jnp.sum(vectors * vectors, 1, keepdims=True)
        squares[pl.ds(p, 1), :] = jnp.broadcast_to(square, (block_len, 128)).T[:1, :]
        scaled = (vectors * gain[...]).astype(jnp.bfloat16)
        lhs[p] = scaled


def widen(lhs, wide):
    @pl.when(pl.program_id(0) == 0)
    def _():
        vectors = lhs[...].reshape(-1, lhs.shape[-1])
        for half in range(2):
            for i, piece in enumerate(spread(vectors, half)):
                lanes = slice(i * 256, (i + 1) * 256)
                wide[half, :, :, :, lanes] = piece.reshape(lhs.shape[:-1] + (256,))


def send_kernel(lhs, weights, out, wide):
    widen(lhs, wide)
    product = times(wide, weights)
    out[...] = product.astype(jnp.bfloat16).reshape(out.shape)


def keep_kernel(lhs, weights, got, send, keep, wide):
    widen(lhs, wide)
    product = times(wide, weights).reshape(got.shape)
    summed = (product + got[...].astype(jnp.float32)).astype(jnp.bfloat16)
    high, low = send.shape[1], send.shape[2]
    summed = summed.reshape((2, high, 2, low) + got.shape[-2:])
    send[...] = summed[:, :, 0]
    keep[...] = summed[:, :, 1]


def times(lhs, weights):
    depth = lhs.shape[-1]
    return jnp.dot(
        lhs[...].reshape(-1, depth),
        weights[...].reshape(depth, weights.shape[-1]),
        preferred_element_type=jnp.float32,
    )


def vmem_call(kernel, n_in, out_shape, scratch, flops):
    whole = pl.BlockSpec(memory_space=pltpu.VMEM)
    return pl.pallas_call(
        kernel,
        in_specs=[pl.BlockSpec(memory_space=pltpu.SMEM)] + [whole] * n_in,
        out_specs=jax.tree.map(lambda _: whole, out_shape),
        out_shape=out_shape,
        scratch_shapes=scratch,
        compiler_params=pltpu.CompilerParams(vmem_limit_bytes=48 << 20),
        cost_estimate=pl.CostEstimate(flops=1, bytes_accessed=1, transcendentals=0),
    )


def gather_near(own, size, index):
    twin = [(r, r ^ 1) for r in range(size)]
    far = []
    for shift in range(1, size // 2):
        pairs = [(r, (r + 2 * shift) % size) for r in range(size)]
        far.append((lax.ppermute(own, "req", pairs), (index - 2 * shift) % size))
    return [(own, index), (lax.ppermute(own, "req", twin), index ^ 1)], far


def gather_far(far, size):
    twin = [(r, r ^ 1) for r in range(size)]
    return far + [(lax.ppermute(part, "req", twin), origin ^ 1) for part, origin in far]


def on_device(
    queries,
    suffix_key_value,
    residual,
    gain,
    gate_up,
    prefix_cache_slots,
    prefix_page_slots,
    lengths,
    counts,
):
    blocks = lax.axis_size("blk")
    groups = lax.axis_size("req")
    column = lax.axis_index("blk")
    group_index = lax.axis_index("req")
    group_len = queries.shape[0]
    heads_kv = suffix_key_value.shape[1]
    head_dim = suffix_key_value.shape[2] // 2
    heads_here = queries.shape[1] // head_dim
    slots_here, page_len = prefix_cache_slots.shape[:2]
    score_scale = math.log2(math.e) / math.sqrt(head_dim)
    kv_head = column * heads_kv // blocks
    page_count = counts[group_index]

    halves = 1
    half_slots = slots_here // halves
    near, far = [], []
    for i in range(halves):
        own_slots = lax.dynamic_slice(
            prefix_cache_slots,
            (i * half_slots, 0, kv_head, 0),
            (half_slots, page_len, 1, 2 * head_dim),
        )
        own_slots = own_slots.reshape(half_slots * page_len, 2 * head_dim)
        near_here, far_here = gather_near(own_slots, groups, group_index)
        near.append(near_here)
        far.append(far_here)

    def interleaved(lists):
        return [part for together in zip(*lists) for part in together]

    request, offset, positions = suffix_layout(
        lengths[group_index], page_count, group_len, page_len
    )
    cosines, sines = rope_tables(positions, head_dim // 2)
    own_head = lax.dynamic_index_in_dim(suffix_key_value, kv_head, 1, keepdims=False)
    allowed = (request[:, None] == request[None, :]) & (offset[None, :] <= offset[:, None])
    mask = jnp.where(allowed, 0.0, NEGATIVE).astype(jnp.float32)

    pages_total = prefix_page_slots.shape[0]
    page_ids = jnp.arange(pages_total, dtype=jnp.int32)
    match = prefix_page_slots[None, :] == page_ids[:, None]
    page_of_slot = jnp.sum(jnp.where(match, page_ids[None, :], 0), 1).reshape(groups, slots_here)

    def meta(parts):
        ids = [
            lax.dynamic_index_in_dim(page_of_slot, o, 0, keepdims=False)
            for _, o in parts[::halves]
        ]
        return jnp.concatenate([page_count[None]] + ids)

    rows = heads_here * group_len
    state = (
        jax.ShapeDtypeStruct((rows, head_dim), jnp.float32),
        jax.ShapeDtypeStruct((rows, head_dim), jnp.float32),
        jax.ShapeDtypeStruct((rows, head_dim), jnp.float32),
    )
    key_flops = 4 * rows * head_dim * slots_here * page_len
    near = interleaved(near)
    settings = (halves, heads_here, head_dim, page_len, score_scale)
    query, acc, top, total, both_new = vmem_call(
        functools.partial(first_kernel, len(near), *settings),
        5 + len(near),
        (jax.ShapeDtypeStruct((rows, head_dim), jnp.bfloat16),)
        + state
        + (jax.ShapeDtypeStruct((group_len, 2 * head_dim), jnp.bfloat16),),
        [],
        key_flops * len(near),
    )(meta(near), queries, own_head, cosines, sines, mask, *[part for part, _ in near])
    arrived = lax.optimization_barrier(([[part for part, _ in parts] for parts in far], top))[0]
    far = interleaved(
        [
            gather_far([(part, origin) for part, (_, origin) in zip(here, parts)], groups)
            for here, parts in zip(arrived, far)
        ]
    )
    stream = vmem_call(
        functools.partial(rest_kernel, len(far), *settings),
        5 + len(far),
        jax.ShapeDtypeStruct((group_len, heads_here * head_dim), jnp.bfloat16),
        [pltpu.VMEM((rows, head_dim), jnp.float32)] * 3,
        key_flops * len(far),
    )(meta(far), query, acc, top, total, residual, *[part for part, _ in far])

    lane_width = 2 * heads_kv * head_dim // blocks
    updated_cache = lax.dynamic_slice_in_dim(
        both_new, column * lane_width % (2 * head_dim), lane_width, 1
    )

    near, far = gather_near(stream, groups, group_index)
    streams = near + gather_far(far, groups)
    features = stream.shape[1]
    bits = blocks.bit_length() - 1
    block_len = groups * group_len // blocks
    lhs, squares = vmem_call(
        functools.partial(lhs_kernel, groups, blocks),
        1 + groups,
        (
            jax.ShapeDtypeStruct((blocks, block_len, features), jnp.bfloat16),
            jax.ShapeDtypeStruct((blocks, block_len), jnp.float32),
        ),
        [pltpu.VMEM((blocks, block_len, features), jnp.bfloat16)],
        8 * groups * group_len * features * 128,
    )(
        jnp.stack([column] + [origin for _, origin in streams]),
        gain[None, :],
        *[part for part, _ in streams],
    )

    def swap(array, bit):
        return lax.ppermute(array, "blk", [(b, b ^ (1 << bit)) for b in range(blocks)])

    def halves(array, bit, left, lead):
        low = sum(1 for other in left if other < bit)
        shape = array.shape[:lead] + (-1, 2, 1 << low) + array.shape[lead + 1 :]
        split = array.reshape(shape)
        out = array.shape[:lead] + (-1,) + array.shape[lead + 1 :]
        return [
            lax.index_in_dim(split, i, lead + 1, keepdims=False).reshape(out) for i in range(2)
        ]

    def add(keep, got):
        return (keep.astype(jnp.float32) + got.astype(jnp.float32)).astype(keep.dtype)

    def multiply(which, bit, begin, end, lhs, got=None, next_bit=None):
        width = end - begin
        tile = 128 * math.gcd(math.gcd(begin // 128, width // 128), 2)
        low = 1 << bit
        high = blocks // (2 * low)
        rows = lhs.reshape(high, 2, low, block_len, features)
        in_specs = [
            pl.BlockSpec(
                (high, None, low, block_len, features), lambda j: (0, which, 0, 0, 0)
            ),
            pl.BlockSpec((features, 2, tile), lambda j: (0, 0, begin // tile + j)),
        ]
        operands = [rows, gate_up]
        if got is None:
            kernel = send_kernel
            out = (2, high * low, block_len, width)
            out_specs = pl.BlockSpec(out[:-1] + (tile,), lambda j: (0, 0, 0, j))
            out_shape = jax.ShapeDtypeStruct(out, jnp.bfloat16)
        else:
            rest = [other for other in range(bits) if other != bit]
            next_low = 1 << sum(1 for other in rest if other < next_bit)
            next_high = high * low // (2 * next_low)
            out = (2, next_high, next_low, block_len, width)
            spec = pl.BlockSpec(out[:-1] + (tile,), lambda j: (0, 0, 0, 0, j))
            kernel = keep_kernel
            in_specs.append(
                pl.BlockSpec((2, high * low, block_len, tile), lambda j: (0, 0, 0, j))
            )
            operands.append(got)
            out_specs = (spec, spec)
            out_shape = (jax.ShapeDtypeStruct(out, jnp.bfloat16),) * 2
        result = pl.pallas_call(
            kernel,
            grid=(width // tile,),
            in_specs=in_specs,
            out_specs=out_specs,
            out_shape=out_shape,
            scratch_shapes=[pltpu.VMEM((2, high, low, block_len, 2 * features), jnp.bfloat16)],
            compiler_params=pltpu.CompilerParams(vmem_limit_bytes=48 << 20),
            cost_estimate=pl.CostEstimate(flops=1, bytes_accessed=1, transcendentals=0),
        )(*operands)
        if got is None:
            return result
        return [part.reshape((2, -1, block_len, width)) for part in result]

    width_here = gate_up.shape[2]
    units = width_here // 128
    whole_units = sum(size for size, _ in CHUNKS)
    bounds, so_far = [0], 0
    for size, _ in CHUNKS:
        so_far += size
        bounds.append(128 * max(bounds[-1] // 128 + 1, units * so_far // whole_units))
    orders = [list(order) + list(range(len(order), bits)) for _, order in CHUNKS]

    pieces = [None] * len(CHUNKS)
    flying, kept, lefts = {}, {}, {}
    square_sum, square_keep, square_left = squares, None, list(range(bits))
    token = squares

    def after(array):
        return lax.optimization_barrier((array, token))[0]

    for step in STEPS:
        kind, c = step[0], int(step[1:])
        if kind == "Q":
            if c == 0:
                square_sum = after(squares)
            else:
                square_sum = add(after(square_keep), flying["Q"])
                square_left.remove(c - 1)
            for bit in [c] if c < 2 else range(c, bits):
                if bit > c:
                    square_sum = add(square_keep, flying["Q"])
                    square_left.remove(bit - 1)
                send, square_keep = halves(square_sum, bit, square_left, 0)
                flying["Q"] = swap(send, bit)
            token = square_sum
            continue
        begin, end, order = bounds[c], bounds[c + 1], orders[c]
        if kind == "S":
            send = multiply(0, order[0], begin, end, after(lhs))
            lefts[c] = list(range(bits))
            flying[c] = swap(send, order[0])
            token = send
        elif kind == "K":
            send, kept[c] = multiply(1, order[0], begin, end, lhs, after(flying[c]), order[1])
            lefts[c].remove(order[0])
            flying[c] = swap(send, order[1])
            token = send
        elif kind == "A":
            for n in range(2, bits):
                summed = add(after(kept[c]), flying[c])
                lefts[c].remove(order[n - 1])
                send, kept[c] = halves(summed, order[n], lefts[c], 1)
                flying[c] = swap(send, order[n])
            token = send
        else:
            summed = after(kept[c]).astype(jnp.float32) + flying[c].astype(jnp.float32)
            norm = lax.rsqrt(
                (square_keep + flying["Q"]).reshape(block_len, 1) / D + EPSILON
            )
            summed = summed.reshape(2, block_len, end - begin) * norm
            pieces[c] = (jax.nn.silu(summed[0]) * summed[1]).astype(jnp.bfloat16)
            token = pieces[c]
    return (jnp.concatenate(pieces, 1), updated_cache)


def solution(mesh):
    placed = (
        P("req", "blk"),
        P("req", None, None),
        P("req", "blk"),
        P("blk"),
        P("blk", None, "req"),
        P("req", None, None, None),
        P(),
        P(),
        P(),
    )
    return jax.shard_map(
        on_device,
        mesh=mesh,
        in_specs=placed,
        out_specs=(P("blk", "req"), P("req", "blk")),
        check_vma=False,
    )
```
